32 devices in a mesh: blk: 8 (over y, x, core), rep: 4 (over z).
Axes of the slice: x: 2, y: 2, z: 4, core: 2. Of those that a mesh axis runs over, the one named last changes fastest.
Arguments:
- features: bfloat16 [8192, 128], P(('blk', 'rep')), may hold values from -6 to 6
- node_degree: int32 [8192], P(('blk', 'rep')), may hold values from 1 to 16
- edge_target: int32 [8, 4, 768], P('blk', 'rep'), may hold values from 0 to 1023
- edge_source: int32 [8, 4, 768], P('blk', 'rep'), may hold values from 0 to 255
- edge_count: int32 [8, 4, 8], P('blk', 'rep'), may hold values from 0 to 96, as said below
- layer_weight: bfloat16 [128, 256], replicated, may hold values from -0.5 to 0.5
- layer_bias: float32 [256], replicated, may hold values from -3 to 3
- cotangent: bfloat16 [8192, 256], P(('blk', 'rep')), may hold values from -0.06591797 to 0.06591797
Outputs:
- hidden: bfloat16 [8192, 256], P(('blk', 'rep'))
- grad_weight: float32 [128, 256], replicated
- grad_bias: float32 [256], replicated
The draws below stay inside these ranges and needn't reach their ends.
Inputs may be any that keep to these rules, and one draw needn't show every extreme that they name: edge_count[b, q, c] is at most 96, and edge_count[b, q, b] equals 96 for every b and q.
All inputs are finite; a program needn't handle non-finite values.
Results may differ from the reference program's by a relative error of at most 0.0058.
Values may be sent and summed in bfloat16 or wider, within the bound.
A program may use at most 64 MiB of HBM per device.

```python
import jax
import jax.numpy as jnp
from jax import lax

F_IN = 128
HID = 256
ROWS_DEV = 1024
EB = 96
NODES = 8192
N_BLK = 8
N_REP = 4


def draw_edge_count(key, part):
    key = jax.random.fold_in(key, 7)
    key_hot, key_raw = jax.random.split(key)
    hot = jax.random.randint(key_hot, (N_BLK, N_REP, 1), 0, 4) == 0
    level = jnp.where(hot, 4, 3).astype(jnp.int32)
    raw = jax.random.randint(key_raw, (N_BLK, N_REP, N_BLK), 0, EB + 1)
    counts = raw * level // 4
    own = jnp.arange(N_BLK, dtype=jnp.int32)[:, None, None] == jnp.arange(N_BLK, dtype=jnp.int32)[None, None, :]
    return jnp.where(own, EB, counts).astype(jnp.int32)


def plant(array, own_key, smallest, high):
    longest = array.shape.index(max(array.shape))
    spots = []
    for shift in (0, 1):
        where = [jax.random.randint(jax.random.fold_in(own_key, axis), (), 0, length) for axis, length in enumerate(array.shape)]
        where[longest] = (where[longest] + shift) % array.shape[longest]
        spots.append(tuple(where))
    return array.at[spots[0]].set(smallest).at[spots[1]].set(high)


def block_scale(rng, dims, pieces, least, largest):
    gain, own = 1.0, jax.random.fold_in(rng, 6)
    for axis_at, blocks in pieces:
        heights = jnp.exp(jax.random.uniform(jax.random.fold_in(own, axis_at), (blocks,), jnp.float32, least / len(pieces), largest / len(pieces)))
        gain = gain * jnp.repeat(heights, dims[axis_at] // blocks).reshape([-1 if axis == axis_at else 1 for axis in range(len(dims))])
    return gain


def bell_draw(own_key, shape, spread, bound, pieces=(), held_as=jnp.bfloat16):
    loudness = block_scale(own_key, shape, pieces, -0.22, 0.18) if pieces else 1.0
    result = jax.random.normal(own_key, shape, jnp.float32) * spread * loudness
    return jnp.minimum(jnp.maximum(result, -bound), bound).astype(held_as)


def setup_inputs(seed: int = 0) -> dict:
    splits = jax.random.split(jax.random.key(seed), 9)
    features = bell_draw(splits[0], (NODES, F_IN), 1.0, 6.0, ((0, 32),))
    node_degree = plant(jax.random.randint(splits[1], (NODES,), 1, 17), jax.random.fold_in(splits[1], 1), 1, 16).astype(jnp.int32)
    edge_target = plant(jax.random.randint(splits[2], (N_BLK, N_REP, N_BLK * EB), 0, ROWS_DEV), jax.random.fold_in(splits[2], 1), 0, ROWS_DEV - 1).astype(jnp.int32)
    edge_source = plant(jax.random.randint(splits[3], (N_BLK, N_REP, N_BLK * EB), 0, ROWS_DEV // N_REP), jax.random.fold_in(splits[3], 1), 0, (ROWS_DEV // N_REP) - 1).astype(jnp.int32)
    edge_count = draw_edge_count(jax.random.fold_in(splits[8], 71), 0)
    layer_weight = bell_draw(splits[5], (F_IN, HID), F_IN ** -0.5, 0.5)
    layer_bias = bell_draw(splits[6], (HID,), 0.5, 3.0, (), jnp.float32)
    cotangent = bell_draw(splits[7], (NODES, HID), (1.0 / (NODES ** 0.5)), 0.06591797, ((0, 32),))
    return dict(features=features, node_degree=node_degree, edge_target=edge_target, edge_source=edge_source, edge_count=edge_count, layer_weight=layer_weight, layer_bias=layer_bias, cotangent=cotangent)


def reference(features, node_degree, edge_target, edge_source, edge_count, layer_weight, layer_bias, cotangent):
    inv_root = lax.rsqrt(node_degree.astype(jnp.float32))
    scaled = (features.astype(jnp.float32) * inv_root[:, None]).astype(jnp.bfloat16)
    quarter = ROWS_DEV // N_REP
    slot_index = jnp.arange(N_BLK * EB, dtype=jnp.int32)
    slot_block = slot_index // EB
    slot_within = slot_index % EB
    rep_index = jnp.arange(N_REP, dtype=jnp.int32)

    def per_block(block_id):
        targets = edge_target[block_id]
        sources = edge_source[block_id]
        counts = edge_count[block_id]
        live = slot_within[None, :] < counts[:, slot_block]
        global_src = slot_block[None, :] * ROWS_DEV + rep_index[:, None] * quarter + sources
        rows = scaled[global_src.reshape(-1)].astype(jnp.float32) * live.reshape(-1)[:, None].astype(jnp.float32)
        return jax.ops.segment_sum(rows, targets.reshape(-1), num_segments=ROWS_DEV)
    gathered = lax.map(per_block, jnp.arange(N_BLK, dtype=jnp.int32)).reshape(NODES, F_IN)
    aggregated = (inv_root[:, None] * (gathered + scaled.astype(jnp.float32))).astype(jnp.bfloat16)
    pre = jnp.dot(aggregated, layer_weight, preferred_element_type=jnp.float32) + layer_bias.astype(jnp.float32)
    hidden = jax.nn.silu(pre).astype(jnp.bfloat16)
    sig = jax.nn.sigmoid(pre)
    grad_pre = cotangent.astype(jnp.float32) * sig * (1.0 + pre * (1.0 - sig))
    grad_pre_b = grad_pre.astype(jnp.bfloat16)
    grad_weight = jnp.dot(aggregated.T, grad_pre_b, preferred_element_type=jnp.float32)
    grad_bias = lax.optimization_barrier(jnp.sum(grad_pre, axis=0))
    return (hidden, grad_weight, grad_bias)
```

```python
import functools

import jax
import jax.numpy as jnp
from jax import lax
from jax.experimental import pallas as pl
from jax.experimental.pallas import tpu as pltpu
from jax.sharding import PartitionSpec as P

MESH = pl.DeviceIdType.MESH
LANES = 128


def layer_kernel(
    feat, deg, tgt, src, cnt, w, bias, cot,
    hid, gw, gb,
    ag, onehot, pick, gt, rs_out, rs_in, g_out, g_in, z_buf, f_buf,
    ag_s, ag_r, rs_s, rs_r, g_s, g_r, z_s, z_r, f_s, f_r,
):
    f32, bf16 = jnp.float32, jnp.bfloat16
    b, q = lax.axis_index("blk"), lax.axis_index("rep")
    blocks, reps = ag.shape[0], z_buf.shape[0]
    quarter, width = feat.shape
    per_block = tgt.shape[-1] // blocks
    core, x, y = lax.rem(b, 2), lax.rem(lax.div(b, 2), 2), lax.div(b, 4)

    def peer(k):
        return (
            lax.rem(core + k % 2, 2)
            + 2 * lax.rem(x + (k // 2) % 2, 2)
            + 4 * lax.rem(y + k // 4, 2)
        )

    def up(k):
        return lax.rem(q + k, reps)

    def push(source, target, send, recv, to_b, to_q):
        return pltpu.make_async_remote_copy(
            src_ref=source, dst_ref=target, send_sem=send, recv_sem=recv,
            device_id=(to_b, to_q), device_id_type=MESH,
        )

    barrier = pltpu.get_barrier_semaphore()
    for k in range(1, blocks):
        pl.semaphore_signal(barrier, inc=1, device_id=(peer(k), q), device_id_type=MESH)
    for k in range(1, reps):
        pl.semaphore_signal(barrier, inc=1, device_id=(b, up(k)), device_id_type=MESH)

    inv_row = lax.rsqrt(deg[...].astype(f32))
    ag[b] = (feat[...].astype(f32).T * inv_row).astype(bf16)

    pl.semaphore_wait(barrier, blocks + reps - 2)

    sends = []
    for k in (6, 2, 4, 1):
        copy = push(ag.at[b], ag.at[b], ag_s.at[k], ag_r.at[b], peer(k), q)
        copy.start()
        sends.append(copy)

    def arrived(k):
        p = peer(k)
        push(ag.at[p], ag.at[p], ag_s.at[k], ag_r.at[p], peer(k), q).wait_recv()

    eye = lax.broadcasted_iota(jnp.int32, (quarter, quarter), 0) == lax.broadcasted_iota(
        jnp.int32, (quarter, quarter), 1
    )
    inv = jnp.sum(jnp.where(eye, inv_row, 0.0), axis=1, keepdims=True)
    scaled = (feat[...].astype(f32) * inv).astype(bf16).astype(f32)

    node = lax.broadcasted_iota(jnp.int32, (quarter, LANES), 0)
    lane = lax.broadcasted_iota(jnp.int32, (1, LANES), 1)
    fill = jnp.full((1, LANES - per_block), -1, jnp.int32)
    for c in range(blocks):
        here = pl.ds(c * LANES, LANES)
        live = lane < cnt[0, :, c : c + 1]
        s_c = jnp.concatenate([src[0, :, c * per_block : (c + 1) * per_block], fill], axis=1)
        t_c = jnp.concatenate([tgt[0, :, c * per_block : (c + 1) * per_block], fill], axis=1)
        t_c = jnp.where(live, t_c, -1)
        pick[c] = jnp.where(node == s_c, 1.0, 0.0).astype(bf16)
        for k in range(reps):
            onehot[k, :, here] = jnp.where(node + up(k) * quarter == t_c, 1.0, 0.0).astype(bf16)

    for k in (2, 4, 6):
        arrived(k)
        p = peer(k)
        copy = push(ag.at[p], ag.at[p], ag_s.at[k + 1], ag_r.at[p], peer(1), q)
        copy.start()
        sends.append(copy)
    for k in (1, 3, 5, 7):
        arrived(k)

    for c in range(blocks):
        rows = jnp.dot(ag[c], pick[c], preferred_element_type=f32)
        gt[:, pl.ds(c * LANES, LANES)] = rows.astype(bf16)

    own = None
    for k in (2, 1, 3, 0):
        part = lax.dot_general(
            onehot[k], gt[...], (((1,), (1,)), ((), ())), preferred_element_type=f32
        )
        if k:
            rs_out[k - 1] = part.astype(bf16)
            copy = push(
                rs_out.at[k - 1], rs_in.at[k - 1], rs_s.at[k - 1], rs_r.at[k - 1], b, up(k)
            )
            copy.start()
            sends.append(copy)
        else:
            own = part + scaled
    for k in (1, 3, 2):
        push(
            rs_out.at[k - 1], rs_in.at[k - 1], rs_s.at[k - 1], rs_r.at[k - 1], b, up(k)
        ).wait_recv()
        own = own + rs_in[k - 1].astype(f32)

    agg = (own * inv).astype(bf16)
    pre = jnp.dot(agg, w[...], preferred_element_type=f32) + bias[...]
    sig = 1.0 / (1.0 + jnp.exp(-pre))
    grad = cot[...].astype(f32) * sig * (1.0 + pre * (1.0 - sig))
    gwl = lax.dot_general(
        agg, grad.astype(bf16), (((0,), (0,)), ((), ())), preferred_element_type=f32
    )
    gbl = jnp.sum(grad, axis=0, keepdims=True)
    step = width // blocks
    hw = gw.shape[1]
    row = lax.broadcasted_iota(jnp.int32, (step, LANES), 0)
    extra = jnp.where(row == 0, gbl[:, :LANES], jnp.where(row == 1, gbl[:, LANES:], 0.0))
    for j in range(blocks):
        g_out[j, :, :hw] = gwl[j * step : (j + 1) * step].astype(bf16)
        g_out[j, :, hw:] = extra.astype(bf16)

    def share(k):
        return push(g_out.at[peer(k)], g_in.at[k - 1], g_s.at[k - 1], g_r.at[k - 1], peer(k), q)

    for k in (6, 7, 2, 3, 4, 5, 1):
        copy = share(k)
        copy.start()
        sends.append(copy)
    hid[...] = (pre * sig).astype(bf16)
    part = g_out[b].astype(f32)
    for k in (1, 2, 3, 4, 5, 6, 7):
        share(k).wait_recv()
        part = part + g_in[k - 1].astype(f32)
    z_buf[q] = part.astype(bf16)
    for k in (2, 1, 3):
        copy = push(z_buf.at[q], z_buf.at[q], z_s.at[k], z_r.at[q], b, up(k))
        copy.start()
        sends.append(copy)
    for k in (1, 3, 2):
        p = up(k)
        push(z_buf.at[p], z_buf.at[p], z_s.at[k], z_r.at[p], b, p).wait_recv()
    part = z_buf[0].astype(f32)
    for k in range(1, reps):
        part = part + z_buf[k].astype(f32)
    f_buf[b] = part.astype(bf16)
    for k in (6, 7, 2, 3, 4, 5, 1):
        copy = push(f_buf.at[b], f_buf.at[b], f_s.at[k], f_r.at[b], peer(k), q)
        copy.start()
        sends.append(copy)
    for k in (1, 2, 3, 4, 5, 6, 7):
        p = peer(k)
        push(f_buf.at[p], f_buf.at[p], f_s.at[k], f_r.at[p], p, q).wait_recv()
    for j in range(blocks):
        gw[j * step : (j + 1) * step, :] = f_buf[j, :, :hw].astype(f32)
    gb[:, :LANES] = f_buf[0, 0:1, hw : hw + LANES].astype(f32)
    gb[:, LANES:] = f_buf[0, 1:2, hw : hw + LANES].astype(f32)
    for copy in sends:
        copy.wait_send()


def fused_per_device(
    features, node_degree, edge_target, edge_source, edge_count, layer_weight, layer_bias, cotangent
):
    quarter, width = features.shape
    blocks, reps = lax.axis_size("blk"), lax.axis_size("rep")
    hw = layer_weight.shape[1]
    step = width // blocks
    bf16 = jnp.bfloat16
    dma = pltpu.SemaphoreType.DMA
    hidden, grad_weight, grad_bias = pl.pallas_call(
        layer_kernel,
        out_shape=(
            jax.ShapeDtypeStruct((quarter, hw), bf16),
            jax.ShapeDtypeStruct((width, hw), jnp.float32),
            jax.ShapeDtypeStruct((1, hw), jnp.float32),
        ),
        in_specs=[pl.BlockSpec(memory_space=pltpu.VMEM)] * 8,
        out_specs=[pl.BlockSpec(memory_space=pltpu.VMEM)] * 3,
        scratch_shapes=[
            pltpu.VMEM((blocks, width, quarter), bf16),
            pltpu.VMEM((reps, quarter, blocks * LANES), bf16),
            pltpu.VMEM((blocks, quarter, LANES), bf16),
            pltpu.VMEM((width, blocks * LANES), bf16),
            pltpu.VMEM((reps - 1, quarter, width), bf16),
            pltpu.VMEM((reps - 1, quarter, width), bf16),
            pltpu.VMEM((blocks, step, hw + LANES), bf16),
            pltpu.VMEM((blocks - 1, step, hw + LANES), bf16),
            pltpu.VMEM((reps, step, hw + LANES), bf16),
            pltpu.VMEM((blocks, step, hw + LANES), bf16),
            dma((blocks,)), dma((blocks,)),
            dma((reps - 1,)), dma((reps - 1,)),
            dma((blocks - 1,)), dma((blocks - 1,)),
            dma((reps,)), dma((reps,)),
            dma((blocks,)), dma((blocks,)),
        ],
        compiler_params=pltpu.CompilerParams(
            collective_id=0, has_side_effects=True, vmem_limit_bytes=24 * 2**20
        ),
    )(
        features, node_degree.reshape(1, quarter), edge_target, edge_source, edge_count,
        layer_weight, layer_bias.reshape(1, hw), cotangent,
    )
    return hidden, grad_weight, grad_bias.reshape(hw)


def per_device(
    features, node_degree, edge_target, edge_source, edge_count, layer_weight, layer_bias, cotangent
):
    quarter = features.shape[0]
    width = features.shape[1]
    blocks = lax.axis_size("blk")
    slots = edge_target.shape[-1]
    per_block = slots // blocks
    row_count = quarter * lax.axis_size("rep")
    inv_root = lax.rsqrt(node_degree.astype(jnp.float32))
    scaled = (features.astype(jnp.float32) * inv_root[:, None]).astype(jnp.bfloat16)
    targets = edge_target.reshape(slots)
    sources = edge_source.reshape(slots)
    counts = edge_count.reshape(blocks)
    live = (jnp.arange(per_block, dtype=jnp.int32)[None, :] < counts[:, None]).reshape(slots)
    slot_block = jnp.arange(slots, dtype=jnp.int32) // per_block
    source_index = slot_block * quarter + sources
    empty = jnp.zeros((row_count, width), jnp.float32)
    piece = lax.all_gather(scaled, "blk", axis=0, tiled=True)
    length = piece.shape[0]
    usable = live & (source_index >= 0) & (source_index < length)
    rows = piece[jnp.clip(source_index, 0, length - 1)].astype(jnp.float32) * usable[
        :, None
    ].astype(jnp.float32)
    partial_value = empty.at[targets].add(rows)
    total = lax.psum(partial_value, "rep")
    own_rows = lax.dynamic_slice_in_dim(total, lax.axis_index("rep") * quarter, quarter, 0)
    aggregated = (inv_root[:, None] * (own_rows + scaled.astype(jnp.float32))).astype(jnp.bfloat16)
    pre = jnp.dot(aggregated, layer_weight, preferred_element_type=jnp.float32) + layer_bias
    hidden = jax.nn.silu(pre).astype(jnp.bfloat16)
    sig = jax.nn.sigmoid(pre)
    grad_pre = cotangent.astype(jnp.float32) * sig * (1.0 + pre * (1.0 - sig))
    grad_pre_b = grad_pre.astype(jnp.bfloat16)
    local_weight = jnp.einsum(
        "nf,nh->fh", aggregated, grad_pre_b, preferred_element_type=jnp.float32
    )
    local_bias = jnp.sum(grad_pre, axis=0)
    grad_weight, grad_bias = lax.psum((local_weight, local_bias), ("blk", "rep"))
    return (hidden, grad_weight, grad_bias)


def solution(mesh):
    in_specs = (
        P(("blk", "rep"), None),
        P(("blk", "rep")),
        P("blk", "rep", None),
        P("blk", "rep", None),
        P("blk", "rep", None),
        P(),
        P(),
        P(("blk", "rep"), None),
    )
    out_specs = (P(("blk", "rep"), None), P(), P())
    fused = mesh.shape["blk"] == 8 and mesh.shape["rep"] == 4
    return jax.shard_map(
        fused_per_device if fused else per_device, mesh=mesh, in_specs=in_specs, out_specs=out_specs, check_vma=False
    )
```

```python
import functools

import jax
import jax.numpy as jnp
from jax import lax
from jax.experimental import pallas as pl
from jax.experimental.pallas import tpu as pltpu
from jax.sharding import PartitionSpec as P

MESH = pl.DeviceIdType.MESH
LANES = 128


def layer_kernel(
    feat_h, deg_h, tgt_h, src_h, cnt_h, w_h, bias_h, cot_h,
    hid, gw, gb,
    feat, deg, tgt, src, cnt, w, bias, cot, ag, onehot, pick, gt, rs_out, rs_in, g_out, g_in, z_buf, f_buf,
    in_s, ag_s, ag_r, rs_s, rs_r, g_s, g_r, z_s, z_r, f_s, f_r,
):
    f32, bf16 = jnp.float32, jnp.bfloat16
    b, q = lax.axis_index("blk"), lax.axis_index("rep")
    blocks, reps = ag.shape[0], z_buf.shape[0]
    quarter, width = feat.shape
    per_block = tgt.shape[-1] // blocks
    core, x, y = lax.rem(b, 2), lax.rem(lax.div(b, 2), 2), lax.div(b, 4)

    def peer(k):
        return (
            lax.rem(core + k % 2, 2)
            + 2 * lax.rem(x + (k // 2) % 2, 2)
            + 4 * lax.rem(y + k // 4, 2)
        )

    def up(k):
        return lax.rem(q + k, reps)

    def push(source, target, send, recv, to_b, to_q):
        return pltpu.make_async_remote_copy(
            src_ref=source, dst_ref=target, send_sem=send, recv_sem=recv,
            device_id=(to_b, to_q), device_id_type=MESH,
        )

    loads = [
        pltpu.make_async_copy(source, target, in_s.at[i])
        for i, (source, target) in enumerate((
            (feat_h, feat), (deg_h, deg), (tgt_h, tgt), (src_h, src),
            (cnt_h, cnt), (w_h, w), (bias_h, bias), (cot_h, cot),
        ))
    ]
    for load in loads:
        load.start()

    barrier = pltpu.get_barrier_semaphore()
    for k in range(1, blocks):
        pl.semaphore_signal(barrier, inc=1, device_id=(peer(k), q), device_id_type=MESH)
    for k in range(1, reps):
        pl.semaphore_signal(barrier, inc=1, device_id=(b, up(k)), device_id_type=MESH)

    loads[0].wait()
    loads[1].wait()
    inv_row = lax.rsqrt(deg[...].astype(f32))
    ag[b] = (feat[...].astype(f32).T * inv_row).astype(bf16)

    pl.semaphore_wait(barrier, blocks + reps - 2)

    sends = []
    for k in (6, 2, 4, 1):
        copy = push(ag.at[b], ag.at[b], ag_s.at[k], ag_r.at[b], peer(k), q)
        copy.start()
        sends.append(copy)

    def arrived(k):
        p = peer(k)
        push(ag.at[p], ag.at[p], ag_s.at[k], ag_r.at[p], peer(k), q).wait_recv()

    eye = lax.broadcasted_iota(jnp.int32, (quarter, quarter), 0) == lax.broadcasted_iota(
        jnp.int32, (quarter, quarter), 1
    )
    inv = jnp.sum(jnp.where(eye, inv_row, 0.0), axis=1, keepdims=True)
    scaled = (feat[...].astype(f32) * inv).astype(bf16).astype(f32)

    for load in loads[2:]:
        load.wait()
    node = lax.broadcasted_iota(jnp.int32, (quarter, LANES), 0)
    lane = lax.broadcasted_iota(jnp.int32, (1, LANES), 1)
    fill = jnp.full((1, LANES - per_block), -1, jnp.int32)
    for c in range(blocks):
        here = pl.ds(c * LANES, LANES)
        live = lane < cnt[0, :, c : c + 1]
        s_c = jnp.concatenate([src[0, :, c * per_block : (c + 1) * per_block], fill], axis=1)
        t_c = jnp.concatenate([tgt[0, :, c * per_block : (c + 1) * per_block], fill], axis=1)
        t_c = jnp.where(live, t_c, -1)
        pick[c] = jnp.where(node == s_c, 1.0, 0.0).astype(bf16)
        for k in range(reps):
            onehot[k, :, here] = jnp.where(node + up(k) * quarter == t_c, 1.0, 0.0).astype(bf16)

    for k in (2, 4, 6):
        arrived(k)
        p = peer(k)
        copy = push(ag.at[p], ag.at[p], ag_s.at[k + 1], ag_r.at[p], peer(1), q)
        copy.start()
        sends.append(copy)
    for k in (1, 3, 5, 7):
        arrived(k)

    for c in range(blocks):
        rows = jnp.dot(ag[c], pick[c], preferred_element_type=f32)
        gt[:, pl.ds(c * LANES, LANES)] = rows.astype(bf16)

    own = None
    for k in (2, 1, 3, 0):
        part = lax.dot_general(
            onehot[k], gt[...], (((1,), (1,)), ((), ())), preferred_element_type=f32
        )
        if k:
            rs_out[k - 1] = part.astype(bf16)
            copy = push(
                rs_out.at[k - 1], rs_in.at[k - 1], rs_s.at[k - 1], rs_r.at[k - 1], b, up(k)
            )
            copy.start()
            sends.append(copy)
        else:
            own = part + scaled
    for k in (1, 3, 2):
        push(
            rs_out.at[k - 1], rs_in.at[k - 1], rs_s.at[k - 1], rs_r.at[k - 1], b, up(k)
        ).wait_recv()
        own = own + rs_in[k - 1].astype(f32)

    agg = (own * inv).astype(bf16)
    pre = jnp.dot(agg, w[...], preferred_element_type=f32) + bias[...]
    sig = 1.0 / (1.0 + jnp.exp(-pre))
    grad = cot[...].astype(f32) * sig * (1.0 + pre * (1.0 - sig))
    gwl = lax.dot_general(
        agg, grad.astype(bf16), (((0,), (0,)), ((), ())), preferred_element_type=f32
    )
    gbl = jnp.sum(grad, axis=0, keepdims=True)
    step = width // blocks
    hw = gw.shape[1]
    row = lax.broadcasted_iota(jnp.int32, (step, LANES), 0)
    extra = jnp.where(row == 0, gbl[:, :LANES], jnp.where(row == 1, gbl[:, LANES:], 0.0))
    for j in range(blocks):
        g_out[j, :, :hw] = gwl[j * step : (j + 1) * step].astype(bf16)
        g_out[j, :, hw:] = extra.astype(bf16)

    def share(k):
        return push(g_out.at[peer(k)], g_in.at[k - 1], g_s.at[k - 1], g_r.at[k - 1], peer(k), q)

    for k in (6, 7, 2, 3, 4, 5, 1):
        copy = share(k)
        copy.start()
        sends.append(copy)
    hid[...] = (pre * sig).astype(bf16)
    part = g_out[b].astype(f32)
    for k in (1, 2, 3, 4, 5, 6, 7):
        share(k).wait_recv()
        part = part + g_in[k - 1].astype(f32)
    z_buf[q] = part.astype(bf16)
    for k in (2, 1, 3):
        copy = push(z_buf.at[q], z_buf.at[q], z_s.at[k], z_r.at[q], b, up(k))
        copy.start()
        sends.append(copy)
    for k in (1, 3, 2):
        p = up(k)
        push(z_buf.at[p], z_buf.at[p], z_s.at[k], z_r.at[p], b, p).wait_recv()
    part = z_buf[0].astype(f32)
    for k in range(1, reps):
        part = part + z_buf[k].astype(f32)
    f_buf[b] = part.astype(bf16)
    for k in (6, 7, 2, 3, 4, 5, 1):
        copy = push(f_buf.at[b], f_buf.at[b], f_s.at[k], f_r.at[b], peer(k), q)
        copy.start()
        sends.append(copy)
    for k in (1, 2, 3, 4, 5, 6, 7):
        p = peer(k)
        push(f_buf.at[p], f_buf.at[p], f_s.at[k], f_r.at[p], p, q).wait_recv()
    for j in range(blocks):
        gw[j * step : (j + 1) * step, :] = f_buf[j, :, :hw].astype(f32)
    gb[:, :LANES] = f_buf[0, 0:1, hw : hw + LANES].astype(f32)
    gb[:, LANES:] = f_buf[0, 1:2, hw : hw + LANES].astype(f32)
    for copy in sends:
        copy.wait_send()


def write_kernel(hid, gw, gb, hid_h, gw_h, gb_h, sems):
    copies = [
        pltpu.make_async_copy(source, target, sems.at[i])
        for i, (source, target) in enumerate(((hid, hid_h), (gw, gw_h), (gb, gb_h)))
    ]
    for copy in copies:
        copy.start()
    for copy in copies:
        copy.wait()


def fused_per_device(
    features, node_degree, edge_target, edge_source, edge_count, layer_weight, layer_bias, cotangent
):
    quarter, width = features.shape
    blocks, reps = lax.axis_size("blk"), lax.axis_size("rep")
    hw = layer_weight.shape[1]
    step = width // blocks
    bf16 = jnp.bfloat16
    dma = pltpu.SemaphoreType.DMA
    def hbm(array):
        return pltpu.with_memory_space_constraint(array, pltpu.HBM)

    hidden, grad_weight, grad_bias = pl.pallas_call(
        layer_kernel,
        out_shape=(
            jax.ShapeDtypeStruct((quarter, hw), bf16),
            jax.ShapeDtypeStruct((width, hw), jnp.float32),
            jax.ShapeDtypeStruct((1, hw), jnp.float32),
        ),
        in_specs=[pl.BlockSpec(memory_space=pltpu.HBM)] * 8,
        out_specs=[pl.BlockSpec(memory_space=pltpu.VMEM)] * 3,
        scratch_shapes=[
            pltpu.VMEM((quarter, width), bf16),
            pltpu.VMEM((1, quarter), jnp.int32),
            pltpu.VMEM(edge_target.shape, jnp.int32),
            pltpu.VMEM(edge_source.shape, jnp.int32),
            pltpu.VMEM(edge_count.shape, jnp.int32),
            pltpu.VMEM((width, hw), bf16),
            pltpu.VMEM((1, hw), jnp.float32),
            pltpu.VMEM((quarter, hw), bf16),
            pltpu.VMEM((blocks, width, quarter), bf16),
            pltpu.VMEM((reps, quarter, blocks * LANES), bf16),
            pltpu.VMEM((blocks, quarter, LANES), bf16),
            pltpu.VMEM((width, blocks * LANES), bf16),
            pltpu.VMEM((reps - 1, quarter, width), bf16),
            pltpu.VMEM((reps - 1, quarter, width), bf16),
            pltpu.VMEM((blocks, step, hw + LANES), bf16),
            pltpu.VMEM((blocks - 1, step, hw + LANES), bf16),
            pltpu.VMEM((reps, step, hw + LANES), bf16),
            pltpu.VMEM((blocks, step, hw + LANES), bf16),
            dma((8,)),
            dma((blocks,)), dma((blocks,)),
            dma((reps - 1,)), dma((reps - 1,)),
            dma((blocks - 1,)), dma((blocks - 1,)),
            dma((reps,)), dma((reps,)),
            dma((blocks,)), dma((blocks,)),
        ],
        compiler_params=pltpu.CompilerParams(
            collective_id=0, has_side_effects=True, vmem_limit_bytes=24 * 2**20
        ),
    )(
        hbm(features), hbm(node_degree.reshape(1, quarter)), hbm(edge_target), hbm(edge_source),
        hbm(edge_count), hbm(layer_weight), hbm(layer_bias.reshape(1, hw)), hbm(cotangent),
    )
    hidden, grad_weight, grad_bias = pl.pallas_call(
        write_kernel,
        out_shape=(
            jax.ShapeDtypeStruct((quarter, hw), bf16),
            jax.ShapeDtypeStruct((width, hw), jnp.float32),
            jax.ShapeDtypeStruct((1, hw), jnp.float32),
        ),
        in_specs=[pl.BlockSpec(memory_space=pltpu.VMEM)] * 3,
        out_specs=[pl.BlockSpec(memory_space=pltpu.HBM)] * 3,
        scratch_shapes=[dma((3,))],
    )(hidden, grad_weight, grad_bias)
    return hidden, grad_weight, grad_bias.reshape(hw)


def per_device(
    features, node_degree, edge_target, edge_source, edge_count, layer_weight, layer_bias, cotangent
):
    quarter = features.shape[0]
    width = features.shape[1]
    blocks = lax.axis_size("blk")
    slots = edge_target.shape[-1]
    per_block = slots // blocks
    row_count = quarter * lax.axis_size("rep")
    inv_root = lax.rsqrt(node_degree.astype(jnp.float32))
    scaled = (features.astype(jnp.float32) * inv_root[:, None]).astype(jnp.bfloat16)
    targets = edge_target.reshape(slots)
    sources = edge_source.reshape(slots)
    counts = edge_count.reshape(blocks)
    live = (jnp.arange(per_block, dtype=jnp.int32)[None, :] < counts[:, None]).reshape(slots)
    slot_block = jnp.arange(slots, dtype=jnp.int32) // per_block
    source_index = slot_block * quarter + sources
    empty = jnp.zeros((row_count, width), jnp.float32)
    piece = lax.all_gather(scaled, "blk", axis=0, tiled=True)
    length = piece.shape[0]
    usable = live & (source_index >= 0) & (source_index < length)
    rows = piece[jnp.clip(source_index, 0, length - 1)].astype(jnp.float32) * usable[
        :, None
    ].astype(jnp.float32)
    partial_value = empty.at[targets].add(rows)
    total = lax.psum(partial_value, "rep")
    own_rows = lax.dynamic_slice_in_dim(total, lax.axis_index("rep") * quarter, quarter, 0)
    aggregated = (inv_root[:, None] * (own_rows + scaled.astype(jnp.float32))).astype(jnp.bfloat16)
    pre = jnp.dot(aggregated, layer_weight, preferred_element_type=jnp.float32) + layer_bias
    hidden = jax.nn.silu(pre).astype(jnp.bfloat16)
    sig = jax.nn.sigmoid(pre)
    grad_pre = cotangent.astype(jnp.float32) * sig * (1.0 + pre * (1.0 - sig))
    grad_pre_b = grad_pre.astype(jnp.bfloat16)
    local_weight = jnp.einsum(
        "nf,nh->fh", aggregated, grad_pre_b, preferred_element_type=jnp.float32
    )
    local_bias = jnp.sum(grad_pre, axis=0)
    grad_weight, grad_bias = lax.psum((local_weight, local_bias), ("blk", "rep"))
    return (hidden, grad_weight, grad_bias)


def solution(mesh):
    in_specs = (
        P(("blk", "rep"), None),
        P(("blk", "rep")),
        P("blk", "rep", None),
        P("blk", "rep", None),
        P("blk", "rep", None),
        P(),
        P(),
        P(("blk", "rep"), None),
    )
    out_specs = (P(("blk", "rep"), None), P(), P())
    fused = mesh.shape["blk"] == 8 and mesh.shape["rep"] == 4
    return jax.shard_map(
        fused_per_device if fused else per_device, mesh=mesh, in_specs=in_specs, out_specs=out_specs, check_vma=False
    )
```

```python
import functools

import jax
import jax.numpy as jnp
from jax import lax
from jax.experimental import pallas as pl
from jax.experimental.pallas import tpu as pltpu
from jax.sharding import PartitionSpec as P

MESH = pl.DeviceIdType.MESH
LANES = 128


def layer_kernel(
    feat_h, deg_h, tgt_h, src_h, cnt_h, w_h, bias_h, cot_h,
    hid, gw, gb,
    feat, deg, tgt, src, cnt, w, bias, cot, ag, onehot, pick, gt, rs_out, rs_in, c_out, c_in, a1, a2, b1, b2, f_out, f_in,
    in_s, ag_s, ag_r, rs_s, rs_r, c_s, c_r, a1_s, a1_r, a2_s, a2_r, b1_s, b1_r, b2_s, b2_r, f_s, f_r,
):
    f32, bf16 = jnp.float32, jnp.bfloat16
    b, q = lax.axis_index("blk"), lax.axis_index("rep")
    blocks, reps = ag.shape[1], onehot.shape[0]
    quarter, width = feat.shape
    half = width // 2
    per_block = tgt.shape[-1] // blocks
    core, x, y = lax.rem(b, 2), lax.rem(lax.div(b, 2), 2), lax.div(b, 4)

    def peer(k):
        return (
            lax.rem(core + k % 2, 2)
            + 2 * lax.rem(x + (k // 2) % 2, 2)
            + 4 * lax.rem(y + k // 4, 2)
        )

    def up(k):
        return lax.rem(q + k, reps)

    def push(source, target, send, recv, to_b, to_q):
        return pltpu.make_async_remote_copy(
            src_ref=source, dst_ref=target, send_sem=send, recv_sem=recv,
            device_id=(to_b, to_q), device_id_type=MESH,
        )

    loads = [
        pltpu.make_async_copy(source, target, in_s.at[i])
        for i, (source, target) in enumerate((
            (feat_h, feat), (deg_h, deg), (tgt_h, tgt), (src_h, src),
            (cnt_h, cnt), (w_h, w), (bias_h, bias), (cot_h, cot),
        ))
    ]
    for load in loads:
        load.start()

    barrier = pltpu.get_barrier_semaphore()
    near = (1, 2, 4, 6)
    for k in near:
        pl.semaphore_signal(barrier, inc=1, device_id=(peer(k), q), device_id_type=MESH)
    for k in range(1, reps):
        pl.semaphore_signal(barrier, inc=1, device_id=(b, up(k)), device_id_type=MESH)

    loads[0].wait()
    loads[1].wait()
    inv_row = lax.rsqrt(deg[...].astype(f32))
    scaled = (feat[...].astype(f32).T * inv_row).astype(bf16)
    for h in range(2):
        ag[h, b] = scaled[h * half : (h + 1) * half]

    pl.semaphore_wait(barrier, len(near) + reps - 1)

    sends = []

    def piece(h, k, p, to_b):
        return push(ag.at[h, p], ag.at[h, p], ag_s.at[h, k], ag_r.at[h, p], to_b, q)

    for h in range(2):
        for k in (6, 2, 4, 1):
            copy = piece(h, k, b, peer(k))
            copy.start()
            sends.append(copy)

    for load in loads[2:]:
        load.wait()
    node = lax.broadcasted_iota(jnp.int32, (quarter, LANES), 0)
    lane = lax.broadcasted_iota(jnp.int32, (1, LANES), 1)
    fill = jnp.full((1, LANES - per_block), -1, jnp.int32)
    for c in range(blocks):
        here = pl.ds(c * LANES, LANES)
        live = lane < cnt[0, :, c : c + 1]
        s_c = jnp.concatenate([src[0, :, c * per_block : (c + 1) * per_block], fill], axis=1)
        t_c = jnp.concatenate([tgt[0, :, c * per_block : (c + 1) * per_block], fill], axis=1)
        t_c = jnp.where(live, t_c, -1)
        pick[c] = jnp.where(node == s_c, 1.0, 0.0).astype(bf16)
        for k in range(reps):
            onehot[k, :, here] = jnp.where(node + up(k) * quarter == t_c, 1.0, 0.0).astype(bf16)

    for h in range(2):
        for k in (2, 4, 6):
            piece(h, k, peer(k), peer(k)).wait_recv()
            copy = piece(h, k + 1, peer(k), peer(1))
            copy.start()
            sends.append(copy)

    def partial(h, k):
        return push(
            rs_out.at[h, k - 1], rs_in.at[h, k - 1], rs_s.at[h, k - 1], rs_r.at[h, k - 1], b, up(k)
        )

    def spread(h, k):
        return lax.dot_general(
            gt[h], onehot[k], (((1,), (1,)), ((), ())), preferred_element_type=f32
        )

    for h in range(2):
        for k in (1, 3, 5, 7):
            piece(h, k, peer(k), peer(k)).wait_recv()
        for c in range(blocks):
            rows = jnp.dot(ag[h, c], pick[c], preferred_element_type=f32)
            gt[h, :, pl.ds(c * LANES, LANES)] = rows.astype(bf16)
        for k in (2, 1, 3):
            rs_out[h, k - 1] = spread(h, k).astype(bf16)
            copy = partial(h, k)
            copy.start()
            sends.append(copy)
    halves = []
    for h in range(2):
        own = spread(h, 0) + ag[h, b].astype(f32)
        for k in (1, 3, 2):
            partial(h, k).wait_recv()
            own = own + rs_in[h, k - 1].astype(f32)
        halves.append((own * inv_row).astype(bf16))
    agg = jnp.concatenate(halves, axis=0)

    pre = lax.dot_general(
        agg, w[...], (((0,), (0,)), ((), ())), preferred_element_type=f32
    ) + bias[...]
    sig = 1.0 / (1.0 + jnp.exp(-pre))
    grad = cot[...].astype(f32) * sig * (1.0 + pre * (1.0 - sig))
    gwl = jnp.dot(agg, grad.astype(bf16), preferred_element_type=f32)
    gbl = jnp.sum(grad, axis=0, keepdims=True)
    hw = gw.shape[1]

    chip, low = lax.div(b, 2), half // 2
    first = core == 0
    mine = jnp.where(first, gwl[:half], gwl[half:])
    c_out[:half] = jnp.where(first, gwl[half:], gwl[:half]).astype(bf16)
    c_out[half:] = jnp.broadcast_to(gbl, (c_out.shape[0] - half, hw)).astype(bf16)

    def pair(k):
        return push(c_out, c_in, c_s, c_r, peer(k), q)

    copy = pair(1)
    copy.start()
    sends.append(copy)
    hid[...] = (pre * sig).astype(bf16)

    def over_plane(buf, sem_s, sem_r, k, p):
        return push(buf.at[p], buf.at[p], sem_s.at[k // 2], sem_r.at[p], peer(k), q)

    def over_rep(buf, sem_s, sem_r, k, p):
        return push(buf.at[p], buf.at[p], sem_s.at[k], sem_r.at[p], b, up(k))

    def send_plane(buf, sem_s, sem_r):
        for k in (6, 2, 4):
            copy = over_plane(buf, sem_s, sem_r, k, chip)
            copy.start()
            sends.append(copy)

    def send_rep(buf, sem_s, sem_r):
        for k in (3, 1, 2):
            copy = over_rep(buf, sem_s, sem_r, k, q)
            copy.start()
            sends.append(copy)

    def sum_plane(buf, sem_s, sem_r):
        for k in (2, 4, 6):
            over_plane(buf, sem_s, sem_r, k, lax.div(peer(k), 2)).wait_recv()
        return sum(buf[p].astype(f32) for p in range(blocks // 2))

    def sum_rep(buf, sem_s, sem_r):
        for k in (1, 3, 2):
            over_rep(buf, sem_s, sem_r, k, up(k)).wait_recv()
        return sum(buf[p].astype(f32) for p in range(reps))

    pair(1).wait_recv()
    mine = mine + c_in[:half].astype(f32)
    a1[chip, :low] = mine[:low].astype(bf16)
    a1[chip, low:] = (c_out[half:].astype(f32) + c_in[half:].astype(f32)).astype(bf16)
    b1[q] = mine[low:].astype(bf16)
    send_rep(b1, b1_s, b1_r)
    send_plane(a1, a1_s, a1_r)
    a2[q] = sum_plane(a1, a1_s, a1_r).astype(bf16)
    send_rep(a2, a2_s, a2_r)
    b2[chip] = sum_rep(b1, b1_s, b1_r).astype(bf16)
    send_plane(b2, b2_s, b2_r)
    part_b = sum_plane(b2, b2_s, b2_r)
    part_a = sum_rep(a2, a2_s, a2_r)
    f_out[:low] = part_a[:low]
    f_out[low:] = part_b

    def swap(k):
        return push(f_out, f_in, f_s, f_r, peer(k), q)

    copy = swap(1)
    copy.start()
    sends.append(copy)
    gb[...] = part_a[low : low + 1]
    gw[pl.ds(pl.multiple_of(core * half, half), half), :] = f_out[...]
    swap(1).wait_recv()
    gw[pl.ds(pl.multiple_of((1 - core) * half, half), half), :] = f_in[...]
    for copy in sends:
        copy.wait_send()


def write_kernel(hid, gw, gb, hid_h, gw_h, gb_h, sems):
    copies = [
        pltpu.make_async_copy(source, target, sems.at[i])
        for i, (source, target) in enumerate(((hid, hid_h), (gw, gw_h), (gb, gb_h)))
    ]
    for copy in copies:
        copy.start()
    for copy in copies:
        copy.wait()


def fused_per_device(
    features, node_degree, edge_target, edge_source, edge_count, layer_weight, layer_bias, cotangent
):
    quarter, width = features.shape
    blocks, reps = lax.axis_size("blk"), lax.axis_size("rep")
    hw = layer_weight.shape[1]
    half = width // 2
    bf16 = jnp.bfloat16
    dma = pltpu.SemaphoreType.DMA
    def hbm(array):
        return pltpu.with_memory_space_constraint(array, pltpu.HBM)

    hidden, grad_weight, grad_bias = pl.pallas_call(
        layer_kernel,
        out_shape=(
            jax.ShapeDtypeStruct((quarter, hw), bf16),
            jax.ShapeDtypeStruct((width, hw), jnp.float32),
            jax.ShapeDtypeStruct((1, hw), jnp.float32),
        ),
        in_specs=[pl.BlockSpec(memory_space=pltpu.HBM)] * 8,
        out_specs=[pl.BlockSpec(memory_space=pltpu.VMEM)] * 3,
        scratch_shapes=[
            pltpu.VMEM((quarter, width), bf16),
            pltpu.VMEM((1, quarter), jnp.int32),
            pltpu.VMEM(edge_target.shape, jnp.int32),
            pltpu.VMEM(edge_source.shape, jnp.int32),
            pltpu.VMEM(edge_count.shape, jnp.int32),
            pltpu.VMEM((width, hw), bf16),
            pltpu.VMEM((1, hw), jnp.float32),
            pltpu.VMEM((quarter, hw), bf16),
            pltpu.VMEM((2, blocks, width // 2, quarter), bf16),
            pltpu.VMEM((reps, quarter, blocks * LANES), bf16),
            pltpu.VMEM((blocks, quarter, LANES), bf16),
            pltpu.VMEM((2, width // 2, blocks * LANES), bf16),
            pltpu.VMEM((2, reps - 1, width // 2, quarter), bf16),
            pltpu.VMEM((2, reps - 1, width // 2, quarter), bf16),
            pltpu.VMEM((half + 16, hw), bf16),
            pltpu.VMEM((half + 16, hw), bf16),
            pltpu.VMEM((blocks // 2, half // 2 + 16, hw), bf16),
            pltpu.VMEM((reps, half // 2 + 16, hw), bf16),
            pltpu.VMEM((reps, half // 2, hw), bf16),
            pltpu.VMEM((blocks // 2, half // 2, hw), bf16),
            pltpu.VMEM((half, hw), jnp.float32),
            pltpu.VMEM((half, hw), jnp.float32),
            dma((8,)),
            dma((2, blocks)), dma((2, blocks)),
            dma((2, reps - 1)), dma((2, reps - 1)),
            dma, dma,
            dma((blocks // 2,)), dma((blocks // 2,)),
            dma((reps,)), dma((reps,)),
            dma((reps,)), dma((reps,)),
            dma((blocks // 2,)), dma((blocks // 2,)),
            dma, dma,
        ],
        compiler_params=pltpu.CompilerParams(
            collective_id=0, has_side_effects=True, vmem_limit_bytes=24 * 2**20
        ),
    )(
        hbm(features), hbm(node_degree.reshape(1, quarter)), hbm(edge_target), hbm(edge_source),
        hbm(edge_count), hbm(layer_weight), hbm(layer_bias.reshape(1, hw)), hbm(cotangent),
    )
    hidden, grad_weight, grad_bias = pl.pallas_call(
        write_kernel,
        out_shape=(
            jax.ShapeDtypeStruct((quarter, hw), bf16),
            jax.ShapeDtypeStruct((width, hw), jnp.float32),
            jax.ShapeDtypeStruct((1, hw), jnp.float32),
        ),
        in_specs=[pl.BlockSpec(memory_space=pltpu.VMEM)] * 3,
        out_specs=[pl.BlockSpec(memory_space=pltpu.HBM)] * 3,
        scratch_shapes=[dma((3,))],
        compiler_params=pltpu.CompilerParams(vmem_limit_bytes=2**20),
    )(hidden, grad_weight, grad_bias)
    return hidden, grad_weight, grad_bias.reshape(hw)


def per_device(
    features, node_degree, edge_target, edge_source, edge_count, layer_weight, layer_bias, cotangent
):
    quarter = features.shape[0]
    width = features.shape[1]
    blocks = lax.axis_size("blk")
    slots = edge_target.shape[-1]
    per_block = slots // blocks
    row_count = quarter * lax.axis_size("rep")
    inv_root = lax.rsqrt(node_degree.astype(jnp.float32))
    scaled = (features.astype(jnp.float32) * inv_root[:, None]).astype(jnp.bfloat16)
    targets = edge_target.reshape(slots)
    sources = edge_source.reshape(slots)
    counts = edge_count.reshape(blocks)
    live = (jnp.arange(per_block, dtype=jnp.int32)[None, :] < counts[:, None]).reshape(slots)
    slot_block = jnp.arange(slots, dtype=jnp.int32) // per_block
    source_index = slot_block * quarter + sources
    empty = jnp.zeros((row_count, width), jnp.float32)
    piece = lax.all_gather(scaled, "blk", axis=0, tiled=True)
    length = piece.shape[0]
    usable = live & (source_index >= 0) & (source_index < length)
    rows = piece[jnp.clip(source_index, 0, length - 1)].astype(jnp.float32) * usable[
        :, None
    ].astype(jnp.float32)
    partial_value = empty.at[targets].add(rows)
    total = lax.psum(partial_value, "rep")
    own_rows = lax.dynamic_slice_in_dim(total, lax.axis_index("rep") * quarter, quarter, 0)
    aggregated = (inv_root[:, None] * (own_rows + scaled.astype(jnp.float32))).astype(jnp.bfloat16)
    pre = jnp.dot(aggregated, layer_weight, preferred_element_type=jnp.float32) + layer_bias
    hidden = jax.nn.silu(pre).astype(jnp.bfloat16)
    sig = jax.nn.sigmoid(pre)
    grad_pre = cotangent.astype(jnp.float32) * sig * (1.0 + pre * (1.0 - sig))
    grad_pre_b = grad_pre.astype(jnp.bfloat16)
    local_weight = jnp.einsum(
        "nf,nh->fh", aggregated, grad_pre_b, preferred_element_type=jnp.float32
    )
    local_bias = jnp.sum(grad_pre, axis=0)
    grad_weight, grad_bias = lax.psum((local_weight, local_bias), ("blk", "rep"))
    return (hidden, grad_weight, grad_bias)


def solution(mesh):
    in_specs = (
        P(("blk", "rep"), None),
        P(("blk", "rep")),
        P("blk", "rep", None),
        P("blk", "rep", None),
        P("blk", "rep", None),
        P(),
        P(),
        P(("blk", "rep"), None),
    )
    out_specs = (P(("blk", "rep"), None), P(), P())
    fused = mesh.shape["blk"] == 8 and mesh.shape["rep"] == 4
    return jax.shard_map(
        fused_per_device if fused else per_device, mesh=mesh, in_specs=in_specs, out_specs=out_specs, check_vma=False
    )
```

```python
import functools

import jax
import jax.numpy as jnp
from jax import lax
from jax.experimental import pallas as pl
from jax.experimental.pallas import tpu as pltpu
from jax.sharding import PartitionSpec as P

MESH = pl.DeviceIdType.MESH
LANES = 128


def layer_kernel(
    feat_h, deg_h, tgt_h, src_h, cnt_h, w_h, bias_h, cot_h,
    hid, gw, gb,
    feat, deg, tgt, src, cnt, w, bias, cot, ag, onehot, pick, gt, rs_out, rs_in, c_out, c_in, a1, a2, b1, b2, f_out, f_in,
    in_s, ag_s, ag_r, rs_s, rs_r, c_s, c_r, a1_s, a1_r, a2_s, a2_r, b1_s, b1_r, b2_s, b2_r, f_s, f_r,
):
    f32, bf16 = jnp.float32, jnp.bfloat16
    b, q = lax.axis_index("blk"), lax.axis_index("rep")
    blocks, reps = ag.shape[1], onehot.shape[0]
    quarter, width = feat.shape
    half = width // 2
    per_block = tgt.shape[-1] // blocks
    core, x, y = lax.rem(b, 2), lax.rem(lax.div(b, 2), 2), lax.div(b, 4)

    def peer(k):
        return (
            lax.rem(core + k % 2, 2)
            + 2 * lax.rem(x + (k // 2) % 2, 2)
            + 4 * lax.rem(y + k // 4, 2)
        )

    def up(k):
        return lax.rem(q + k, reps)

    def push(source, target, send, recv, to_b, to_q):
        return pltpu.make_async_remote_copy(
            src_ref=source, dst_ref=target, send_sem=send, recv_sem=recv,
            device_id=(to_b, to_q), device_id_type=MESH,
        )

    loads = [
        pltpu.make_async_copy(source, target, in_s.at[i])
        for i, (source, target) in enumerate((
            (feat_h, feat), (deg_h, deg), (tgt_h, tgt), (src_h, src),
            (cnt_h, cnt), (w_h, w), (bias_h, bias), (cot_h, cot),
        ))
    ]
    for load in loads:
        load.start()

    barrier = pltpu.get_barrier_semaphore()
    near = (1, 2, 4, 6)
    for k in near:
        pl.semaphore_signal(barrier, inc=1, device_id=(peer(k), q), device_id_type=MESH)
    for k in range(1, reps):
        pl.semaphore_signal(barrier, inc=1, device_id=(b, up(k)), device_id_type=MESH)

    loads[0].wait()
    loads[1].wait()
    inv_row = lax.rsqrt(deg[...].astype(f32))
    scaled = (feat[...].astype(f32).T * inv_row).astype(bf16)
    for h in range(2):
        ag[h, b] = scaled[h * half : (h + 1) * half]

    pl.semaphore_wait(barrier, len(near) + reps - 1)

    sends = []

    def piece(h, k, p, to_b):
        return push(ag.at[h, p], ag.at[h, p], ag_s.at[h, k], ag_r.at[h, p], to_b, q)

    for h in range(2):
        for k in (6, 2, 4):
            copy = piece(h, k, b, peer(k))
            copy.start()
            sends.append(copy)
    for h in range(2):
        copy = piece(h, 1, b, peer(1))
        copy.start()
        sends.append(copy)

    for load in loads[2:]:
        load.wait()
    node = lax.broadcasted_iota(jnp.int32, (quarter, LANES), 0)
    target = lax.broadcasted_iota(jnp.int32, (LANES, quarter), 1)
    lane = lax.broadcasted_iota(jnp.int32, (1, LANES), 1)
    fill = jnp.full((1, LANES - per_block), -1, jnp.int32)
    for c in range(blocks):
        here = pl.ds(c * LANES, LANES)
        live = lane < cnt[0, :, c : c + 1]
        s_c = jnp.concatenate([src[0, :, c * per_block : (c + 1) * per_block], fill], axis=1)
        t_c = jnp.concatenate([tgt[0, :, c * per_block : (c + 1) * per_block], fill], axis=1)
        t_c = jnp.where(live, t_c, -1)
        column = jnp.broadcast_to(t_c.astype(f32), (LANES, LANES)).T.astype(jnp.int32)
        column = jnp.concatenate([column] * (quarter // LANES), axis=1)
        pick[c] = jnp.where(node == s_c, 1.0, 0.0).astype(bf16)
        for k in range(reps):
            onehot[k, here] = jnp.where(column - up(k) * quarter == target, 1.0, 0.0).astype(bf16)

    for h in range(2):
        for k in (2, 4, 6):
            piece(h, k, peer(k), peer(k)).wait_recv()
            copy = piece(h, k + 1, peer(k), peer(1))
            copy.start()
            sends.append(copy)

    def partial(h, k):
        return push(
            rs_out.at[h, k - 1], rs_in.at[h, k - 1], rs_s.at[h, k - 1], rs_r.at[h, k - 1], b, up(k)
        )

    def spread(h, k):
        return jnp.dot(gt[h], onehot[k], preferred_element_type=f32)

    for h in range(2):
        for k in (1, 3, 5, 7):
            piece(h, k, peer(k), peer(k)).wait_recv()
        for c in range(blocks):
            rows = jnp.dot(ag[h, c], pick[c], preferred_element_type=f32)
            gt[h, :, pl.ds(c * LANES, LANES)] = rows.astype(bf16)
        for k in (2, 1, 3):
            rs_out[h, k - 1] = spread(h, k).astype(bf16)
            copy = partial(h, k)
            copy.start()
            sends.append(copy)
    halves = []
    for h in range(2):
        own = spread(h, 0) + ag[h, b].astype(f32)
        for k in (1, 3, 2):
            partial(h, k).wait_recv()
            own = own + rs_in[h, k - 1].astype(f32)
        halves.append((own * inv_row).astype(bf16))
    agg = jnp.concatenate(halves, axis=0)

    pre = lax.dot_general(
        agg, w[...], (((0,), (0,)), ((), ())), preferred_element_type=f32
    ) + bias[...]
    sig = 1.0 / (1.0 + jnp.exp(-pre))
    grad = cot[...].astype(f32) * sig * (1.0 + pre * (1.0 - sig))
    gwl = jnp.dot(agg, grad.astype(bf16), preferred_element_type=f32)
    gbl = jnp.sum(grad, axis=0, keepdims=True)
    hw = gw.shape[1]

    chip, low = lax.div(b, 2), half // 2
    first = core == 0
    mine = jnp.where(first, gwl[:half], gwl[half:])
    c_out[:half] = jnp.where(first, gwl[half:], gwl[:half]).astype(bf16)
    c_out[half:] = jnp.broadcast_to(gbl, (c_out.shape[0] - half, hw)).astype(bf16)

    def pair(k):
        return push(c_out, c_in, c_s, c_r, peer(k), q)

    copy = pair(1)
    copy.start()
    sends.append(copy)
    hid[...] = (pre * sig).astype(bf16)

    def over_plane(buf, sem_s, sem_r, k, p):
        return push(buf.at[p], buf.at[p], sem_s.at[k // 2], sem_r.at[p], peer(k), q)

    def over_rep(buf, sem_s, sem_r, k, p):
        return push(buf.at[p], buf.at[p], sem_s.at[k], sem_r.at[p], b, up(k))

    def send_plane(buf, sem_s, sem_r):
        for k in (6, 2, 4):
            copy = over_plane(buf, sem_s, sem_r, k, chip)
            copy.start()
            sends.append(copy)

    def send_rep(buf, sem_s, sem_r):
        for k in (3, 1, 2):
            copy = over_rep(buf, sem_s, sem_r, k, q)
            copy.start()
            sends.append(copy)

    def sum_plane(buf, sem_s, sem_r):
        for k in (2, 4, 6):
            over_plane(buf, sem_s, sem_r, k, lax.div(peer(k), 2)).wait_recv()
        return sum(buf[p].astype(f32) for p in range(blocks // 2))

    def sum_rep(buf, sem_s, sem_r):
        for k in (1, 3, 2):
            over_rep(buf, sem_s, sem_r, k, up(k)).wait_recv()
        return sum(buf[p].astype(f32) for p in range(reps))

    pair(1).wait_recv()
    mine = mine + c_in[:half].astype(f32)
    a1[chip, :low] = mine[:low].astype(bf16)
    a1[chip, low:] = (c_out[half:].astype(f32) + c_in[half:].astype(f32)).astype(bf16)
    b1[q] = mine[low:].astype(bf16)
    send_rep(b1, b1_s, b1_r)
    send_plane(a1, a1_s, a1_r)
    a2[q] = sum_plane(a1, a1_s, a1_r).astype(bf16)
    send_rep(a2, a2_s, a2_r)
    b2[chip] = sum_rep(b1, b1_s, b1_r).astype(bf16)
    send_plane(b2, b2_s, b2_r)
    part_b = sum_plane(b2, b2_s, b2_r)
    part_a = sum_rep(a2, a2_s, a2_r)
    f_out[:low] = part_a[:low]
    f_out[low:] = part_b

    def swap(k):
        return push(f_out, f_in, f_s, f_r, peer(k), q)

    copy = swap(1)
    copy.start()
    sends.append(copy)
    gb[...] = part_a[low : low + 1]
    gw[pl.ds(pl.multiple_of(core * half, half), half), :] = f_out[...]
    swap(1).wait_recv()
    gw[pl.ds(pl.multiple_of((1 - core) * half, half), half), :] = f_in[...]
    for copy in sends:
        copy.wait_send()


def write_kernel(hid, gw, gb, hid_h, gw_h, gb_h, sems):
    copies = [
        pltpu.make_async_copy(source, target, sems.at[i])
        for i, (source, target) in enumerate(((hid, hid_h), (gw, gw_h), (gb, gb_h)))
    ]
    for copy in copies:
        copy.start()
    for copy in copies:
        copy.wait()


def fused_per_device(
    features, node_degree, edge_target, edge_source, edge_count, layer_weight, layer_bias, cotangent
):
    quarter, width = features.shape
    blocks, reps = lax.axis_size("blk"), lax.axis_size("rep")
    hw = layer_weight.shape[1]
    half = width // 2
    bf16 = jnp.bfloat16
    dma = pltpu.SemaphoreType.DMA
    def hbm(array):
        return pltpu.with_memory_space_constraint(array, pltpu.HBM)

    hidden, grad_weight, grad_bias = pl.pallas_call(
        layer_kernel,
        out_shape=(
            jax.ShapeDtypeStruct((quarter, hw), bf16),
            jax.ShapeDtypeStruct((width, hw), jnp.float32),
            jax.ShapeDtypeStruct((1, hw), jnp.float32),
        ),
        in_specs=[pl.BlockSpec(memory_space=pltpu.HBM)] * 8,
        out_specs=[pl.BlockSpec(memory_space=pltpu.VMEM)] * 3,
        scratch_shapes=[
            pltpu.VMEM((quarter, width), bf16),
            pltpu.VMEM((1, quarter), jnp.int32),
            pltpu.VMEM(edge_target.shape, jnp.int32),
            pltpu.VMEM(edge_source.shape, jnp.int32),
            pltpu.VMEM(edge_count.shape, jnp.int32),
            pltpu.VMEM((width, hw), bf16),
            pltpu.VMEM((1, hw), jnp.float32),
            pltpu.VMEM((quarter, hw), bf16),
            pltpu.VMEM((2, blocks, width // 2, quarter), bf16),
            pltpu.VMEM((reps, blocks * LANES, quarter), bf16),
            pltpu.VMEM((blocks, quarter, LANES), bf16),
            pltpu.VMEM((2, width // 2, blocks * LANES), bf16),
            pltpu.VMEM((2, reps - 1, width // 2, quarter), bf16),
            pltpu.VMEM((2, reps - 1, width // 2, quarter), bf16),
            pltpu.VMEM((half + 16, hw), bf16),
            pltpu.VMEM((half + 16, hw), bf16),
            pltpu.VMEM((blocks // 2, half // 2 + 16, hw), bf16),
            pltpu.VMEM((reps, half // 2 + 16, hw), bf16),
            pltpu.VMEM((reps, half // 2, hw), bf16),
            pltpu.VMEM((blocks // 2, half // 2, hw), bf16),
            pltpu.VMEM((half, hw), jnp.float32),
            pltpu.VMEM((half, hw), jnp.float32),
            dma((8,)),
            dma((2, blocks)), dma((2, blocks)),
            dma((2, reps - 1)), dma((2, reps - 1)),
            dma, dma,
            dma((blocks // 2,)), dma((blocks // 2,)),
            dma((reps,)), dma((reps,)),
            dma((reps,)), dma((reps,)),
            dma((blocks // 2,)), dma((blocks // 2,)),
            dma, dma,
        ],
        compiler_params=pltpu.CompilerParams(
            collective_id=0, has_side_effects=True, vmem_limit_bytes=24 * 2**20
        ),
    )(
        hbm(features), hbm(node_degree.reshape(1, quarter)), hbm(edge_target), hbm(edge_source),
        hbm(edge_count), hbm(layer_weight), hbm(layer_bias.reshape(1, hw)), hbm(cotangent),
    )
    hidden, grad_weight, grad_bias = pl.pallas_call(
        write_kernel,
        out_shape=(
            jax.ShapeDtypeStruct((quarter, hw), bf16),
            jax.ShapeDtypeStruct((width, hw), jnp.float32),
            jax.ShapeDtypeStruct((1, hw), jnp.float32),
        ),
        in_specs=[pl.BlockSpec(memory_space=pltpu.VMEM)] * 3,
        out_specs=[pl.BlockSpec(memory_space=pltpu.HBM)] * 3,
        scratch_shapes=[dma((3,))],
        compiler_params=pltpu.CompilerParams(vmem_limit_bytes=2**20),
    )(hidden, grad_weight, grad_bias)
    return hidden, grad_weight, grad_bias.reshape(hw)


def per_device(
    features, node_degree, edge_target, edge_source, edge_count, layer_weight, layer_bias, cotangent
):
    quarter = features.shape[0]
    width = features.shape[1]
    blocks = lax.axis_size("blk")
    slots = edge_target.shape[-1]
    per_block = slots // blocks
    row_count = quarter * lax.axis_size("rep")
    inv_root = lax.rsqrt(node_degree.astype(jnp.float32))
    scaled = (features.astype(jnp.float32) * inv_root[:, None]).astype(jnp.bfloat16)
    targets = edge_target.reshape(slots)
    sources = edge_source.reshape(slots)
    counts = edge_count.reshape(blocks)
    live = (jnp.arange(per_block, dtype=jnp.int32)[None, :] < counts[:, None]).reshape(slots)
    slot_block = jnp.arange(slots, dtype=jnp.int32) // per_block
    source_index = slot_block * quarter + sources
    empty = jnp.zeros((row_count, width), jnp.float32)
    piece = lax.all_gather(scaled, "blk", axis=0, tiled=True)
    length = piece.shape[0]
    usable = live & (source_index >= 0) & (source_index < length)
    rows = piece[jnp.clip(source_index, 0, length - 1)].astype(jnp.float32) * usable[
        :, None
    ].astype(jnp.float32)
    partial_value = empty.at[targets].add(rows)
    total = lax.psum(partial_value, "rep")
    own_rows = lax.dynamic_slice_in_dim(total, lax.axis_index("rep") * quarter, quarter, 0)
    aggregated = (inv_root[:, None] * (own_rows + scaled.astype(jnp.float32))).astype(jnp.bfloat16)
    pre = jnp.dot(aggregated, layer_weight, preferred_element_type=jnp.float32) + layer_bias
    hidden = jax.nn.silu(pre).astype(jnp.bfloat16)
    sig = jax.nn.sigmoid(pre)
    grad_pre = cotangent.astype(jnp.float32) * sig * (1.0 + pre * (1.0 - sig))
    grad_pre_b = grad_pre.astype(jnp.bfloat16)
    local_weight = jnp.einsum(
        "nf,nh->fh", aggregated, grad_pre_b, preferred_element_type=jnp.float32
    )
    local_bias = jnp.sum(grad_pre, axis=0)
    grad_weight, grad_bias = lax.psum((local_weight, local_bias), ("blk", "rep"))
    return (hidden, grad_weight, grad_bias)


def solution(mesh):
    in_specs = (
        P(("blk", "rep"), None),
        P(("blk", "rep")),
        P("blk", "rep", None),
        P("blk", "rep", None),
        P("blk", "rep", None),
        P(),
        P(),
        P(("blk", "rep"), None),
    )
    out_specs = (P(("blk", "rep"), None), P(), P())
    fused = mesh.shape["blk"] == 8 and mesh.shape["rep"] == 4
    return jax.shard_map(
        fused_per_device if fused else per_device, mesh=mesh, in_specs=in_specs, out_specs=out_specs, check_vma=False
    )
```
